256 devices in a mesh: sec: 2 (over x_hi), dp: 16 (over z, core), vocab: 8 (over y, x_lo).
Axes of the slice: x: 4 (x_hi: 2, x_lo: 2; x = x_hi * 2 + x_lo), y: 4, z: 8, core: 2. Of those that a mesh axis runs over, the one named last changes fastest.
Arguments:
- hidden: bfloat16 [768, 5120], P('dp', ('sec', 'vocab')), may hold values from -12 to 12
- head: bfloat16 [5120, 147456], P('sec', ('dp', 'vocab')), may hold values from -1 to 1
- teacher_logits: bfloat16 [768, 147456], P(('sec', 'dp'), 'vocab'), may hold values from -16 to 300
- loss_mask: int32 [768], replicated, may hold values 0 or 1
- token_ids: int32 [768], replicated, may hold values from 0 to 147455
- row_order: int32 [768], replicated, may hold values from 0 to 767, each once
Outputs:
- head_grad: bfloat16 [5120, 147456], P('sec', ('dp', 'vocab'))
- hidden_grad: float32 [768, 5120], P('dp', ('sec', 'vocab'))
- token_kl: float32 [768], P(('sec', 'dp'))
- sampled_gap: float32 [768], P(('sec', 'dp'))
The draws below stay inside these ranges and needn't reach their ends.
Inputs may be any that keep to these rules, and one draw needn't show every extreme that they name: `row_order`: a permutation of 0 to 767.
All inputs are finite; a program needn't handle non-finite values.
Results may differ from the reference program's by a relative error of at most 0.012.
Values may be sent and summed in bfloat16 or wider, within the bound.
No kernel may reach another device: no remote copies, remote signals or barrier semaphores. Data moves between devices by JAX's collectives and lax.ppermute only.
A program may use at most 128 MiB of HBM per device.

```python
import math
import jax
import jax.numpy as jnp
from jax import lax

D = 5120
VOCAB_DEV = 1152
TOKENS = 768
VOCAB = 147456
N_DP = 16
N_VOCAB = 8


def draw_head(key, part):
    key = jax.random.fold_in(key, 11)
    weights = jax.random.truncated_normal(key, -6.0, 6.0, (D, VOCAB), jnp.float32) / math.sqrt(D)
    return weights.astype(jnp.bfloat16)


def draw_hidden(key, part):
    key = jax.random.fold_in(key, 12)
    values = 3.0 * jax.random.truncated_normal(key, -4.0, 4.0, (TOKENS, D), jnp.float32)
    return values.astype(jnp.bfloat16)


def draw_teacher_logits(key, part):
    key = jax.random.fold_in(key, 13)
    values = 3.0 * jax.random.truncated_normal(key, -5.0, 5.0, (TOKENS, VOCAB), jnp.float32)
    return values.astype(jnp.bfloat16)


def touch_ends(entries, own_key, least, largest):
    longest = entries.shape.index(max(entries.shape))
    spots = []
    for shift in (0, 1):
        where = [jax.random.randint(jax.random.fold_in(own_key, axis), (), 0, length) for axis, length in enumerate(entries.shape)]
        where[longest] = (where[longest] + shift) % entries.shape[longest]
        spots.append(tuple(where))
    return entries.at[spots[0]].set(least).at[spots[1]].set(largest)


def setup_inputs(seed: int = 0) -> dict:
    splits = jax.random.split(jax.random.key(seed), 7)
    hidden = draw_hidden(jax.random.fold_in(splits[6], 71), 0)
    head = draw_head(jax.random.fold_in(splits[6], 71), 0)
    teacher_logits = draw_teacher_logits(jax.random.fold_in(splits[6], 71), 0)
    loss_mask = touch_ends((jax.random.randint(splits[3], (TOKENS,), 0, 4) < 3).astype(jnp.int32), jax.random.fold_in(splits[3], 1), 0, 1)
    token_ids = touch_ends(jax.random.randint(splits[4], (TOKENS,), 0, VOCAB), jax.random.fold_in(splits[4], 1), 0, VOCAB - 1).astype(jnp.int32)
    row_order = jax.random.permutation(splits[5], TOKENS).astype(jnp.int32)
    return {"hidden": hidden, "head": head, "teacher_logits": teacher_logits, "loss_mask": loss_mask, "token_ids": token_ids, "row_order": row_order}


def reference(hidden, head, teacher_logits, loss_mask, token_ids, row_order):
    inverse = jnp.argsort(row_order).astype(jnp.int32)
    aligned = jnp.take(teacher_logits, inverse, axis=0)
    weights = loss_mask.astype(jnp.float32)
    block_total = N_DP * N_VOCAB
    block_index = jnp.arange(block_total, dtype=jnp.int32)

    def load_block(index):
        offset = (index * VOCAB_DEV).astype(jnp.int32)
        head_block = lax.dynamic_slice_in_dim(head, offset, VOCAB_DEV, 1)
        teacher_block = lax.dynamic_slice_in_dim(aligned, offset, VOCAB_DEV, 1).astype(jnp.float32)
        logits = jnp.dot(hidden, head_block, preferred_element_type=jnp.float32)
        return offset, head_block, teacher_block, logits

    def first_pass(carry, index):
        max_student, sum_student, max_teacher, sum_teacher, cross_sum, student_pick, teacher_pick = carry
        offset, head_block, teacher_block, logits = load_block(index)
        new_student = jnp.maximum(max_student, jnp.max(logits, axis=1))
        new_teacher = jnp.maximum(max_teacher, jnp.max(teacher_block, axis=1))
        student_scale = jnp.exp(max_student - new_student)
        student_exp = jnp.exp(logits - new_student[:, None])
        sum_student = sum_student * student_scale + jnp.sum(student_exp, axis=1)
        cross_sum = cross_sum * student_scale + jnp.sum(student_exp * (logits - teacher_block), axis=1)
        sum_teacher = sum_teacher * jnp.exp(max_teacher - new_teacher) + jnp.sum(jnp.exp(teacher_block - new_teacher[:, None]), axis=1)
        columns = offset + jnp.arange(VOCAB_DEV, dtype=jnp.int32)
        sampled_hit = columns[None, :] == token_ids[:, None]
        student_pick = student_pick + jnp.sum(jnp.where(sampled_hit, logits, 0.0), axis=1)
        teacher_pick = teacher_pick + jnp.sum(jnp.where(sampled_hit, teacher_block, 0.0), axis=1)
        return (new_student, sum_student, new_teacher, sum_teacher, cross_sum, student_pick, teacher_pick), None

    lowest = jnp.full((TOKENS,), -1e30, jnp.float32)
    zeros = jnp.zeros((TOKENS,), jnp.float32)
    stats, _ = lax.scan(first_pass, (lowest, zeros, lowest, zeros, zeros, zeros, zeros), block_index)
    max_student, sum_student, max_teacher, sum_teacher, cross_sum, student_pick, teacher_pick = stats
    student_lse = max_student + jnp.log(sum_student)
    teacher_lse = max_teacher + jnp.log(sum_teacher)
    token_kl = cross_sum / sum_student - student_lse + teacher_lse
    sampled_gap = (student_pick - student_lse) - (teacher_pick - teacher_lse)

    def second_pass(hidden_total, index):
        offset, head_block, teacher_block, logits = load_block(index)
        log_student = logits - student_lse[:, None]
        log_teacher = teacher_block - teacher_lse[:, None]
        probs = jnp.exp(log_student)
        logit_grad = (weights[:, None] * probs * (log_student - log_teacher - token_kl[:, None])).astype(jnp.bfloat16)
        block_grad = jnp.dot(hidden.T, logit_grad, preferred_element_type=jnp.float32).astype(jnp.bfloat16)
        hidden_total = hidden_total + jnp.dot(logit_grad, head_block.T, preferred_element_type=jnp.float32)
        return hidden_total, block_grad

    hidden_grad, grad_blocks = lax.scan(second_pass, jnp.zeros((TOKENS, D), jnp.float32), block_index)
    head_grad = jnp.transpose(grad_blocks, (1, 0, 2)).reshape(D, VOCAB)
    return head_grad, hidden_grad, token_kl, sampled_gap
```

```python
import jax
import jax.numpy as jnp
from jax import lax
from jax.sharding import PartitionSpec as P

F32 = jnp.float32
BF16 = jnp.bfloat16
NT = (((1,), (1,)), ((), ()))


def merge_stats(table):
    max_s = jnp.max(table[:, 0], axis=0)
    max_t = jnp.max(table[:, 3], axis=0)
    scale_s = jnp.exp(table[:, 0] - max_s[None])
    scale_t = jnp.exp(table[:, 3] - max_t[None])
    return jnp.stack(
        [
            max_s,
            jnp.sum(table[:, 1] * scale_s, axis=0),
            jnp.sum(table[:, 2] * scale_s, axis=0),
            max_t,
            jnp.sum(table[:, 4] * scale_t, axis=0),
            jnp.sum(table[:, 5], axis=0),
            jnp.sum(table[:, 6], axis=0),
        ]
    )


def share(value, axis):
    count = lax.axis_size(axis)
    copies = jnp.broadcast_to(value[None], (count,) + value.shape)
    return lax.all_to_all(copies, axis, split_axis=0, concat_axis=0, tiled=True)


def on_device(hidden, head, teacher_logits, loss_mask, token_ids, row_order):
    dp_size = lax.axis_size("dp")
    vocab_size = lax.axis_size("vocab")
    z_size = dp_size // 2
    sec = lax.axis_index("sec")
    dp = lax.axis_index("dp")
    z, core = dp // 2, dp % 2
    block_width = head.shape[1]
    rows = hidden.shape[0]
    width = hidden.shape[1]
    total_rows = rows * dp_size
    half = total_rows // 2
    teacher_rows = teacher_logits.shape[0]
    swap_sec = [(0, 1), (1, 0)]
    swap_core = [(i, i ^ 1) for i in range(dp_size)]
    z_up = [(i, (i + 2) % dp_size) for i in range(dp_size)]
    z_down = [(i, (i - 2) % dp_size) for i in range(dp_size)]

    features = share(hidden, "vocab").transpose(1, 0, 2).reshape(rows, vocab_size * width)
    all_rows = lax.all_gather(features, "dp", axis=0, tiled=True)

    tiles = teacher_logits.reshape(teacher_rows, dp_size // vocab_size, vocab_size, block_width)
    ordered = lax.all_to_all(
        lax.all_to_all(tiles, "vocab", split_axis=2, concat_axis=1, tiled=True),
        "dp",
        split_axis=1,
        concat_axis=0,
        tiled=True,
    ).reshape(half, block_width)
    arrived = lax.ppermute(ordered, "sec", swap_sec)
    first = sec * half
    my_tokens = first + jnp.arange(half, dtype=jnp.int32)

    def aligned(part, owner):
        order = lax.dynamic_slice_in_dim(row_order, owner * half, half, 0)
        chosen = (order[None, :] == my_tokens[:, None]).astype(BF16)
        return jnp.dot(chosen, part, preferred_element_type=F32)

    teacher_block = aligned(ordered, sec) + aligned(arrived, 1 - sec)

    theirs = lax.dynamic_slice_in_dim(all_rows, (1 - sec) * half, half, 0)
    mine = lax.dynamic_slice_in_dim(all_rows, first, half, 0)
    quarter = half // 2
    sent = [
        lax.ppermute(
            jnp.dot(theirs[i * quarter : (i + 1) * quarter], head, preferred_element_type=F32),
            "sec",
            swap_sec,
        )
        for i in range(2)
    ]
    own = jnp.dot(mine, head, preferred_element_type=F32)
    logits = own + jnp.concatenate(sent, axis=0)

    ids = lax.dynamic_slice_in_dim(token_ids, first, half, 0)
    offset = (dp * vocab_size + lax.axis_index("vocab")) * block_width
    columns = offset + jnp.arange(block_width, dtype=jnp.int32)
    hit = columns[None, :] == ids[:, None]
    top_s = jnp.max(logits, axis=1)
    top_t = jnp.max(teacher_block, axis=1)
    exp_s = jnp.exp(logits - top_s[:, None])
    exp_t = jnp.exp(teacher_block - top_t[:, None])
    local = jnp.stack(
        [
            top_s,
            jnp.sum(exp_s, axis=1),
            jnp.sum(exp_s * (logits - teacher_block), axis=1),
            top_t,
            jnp.sum(exp_t, axis=1),
            jnp.sum(jnp.where(hit, logits, 0.0), axis=1),
            jnp.sum(jnp.where(hit, teacher_block, 0.0), axis=1),
        ]
    )
    stats = merge_stats(share(merge_stats(share(local, "dp")), "vocab"))
    student_lse = stats[0] + jnp.log(stats[1])
    teacher_lse = stats[3] + jnp.log(stats[4])
    token_kl = stats[2] / stats[1] - student_lse + teacher_lse
    sampled_gap = stats[5] - student_lse - (stats[6] - teacher_lse)

    weights = lax.dynamic_slice_in_dim(loss_mask, first, half, 0).astype(F32)
    log_student = logits - student_lse[:, None]
    log_teacher = teacher_block - teacher_lse[:, None]
    my_grad = (
        weights[:, None] * jnp.exp(log_student) * (log_student - log_teacher - token_kl[:, None])
    ).astype(BF16)
    their_grad = lax.ppermute(my_grad, "sec", swap_sec)
    logit_grad = lax.dynamic_update_slice_in_dim(
        jnp.concatenate([their_grad, their_grad], axis=0), my_grad, first, 0
    )

    around = (z + jnp.arange(z_size)) % z_size
    by_chip = jnp.take(logit_grad.reshape(z_size, 2, rows, block_width), around, axis=0)

    def hidden_terms(which):
        part = lax.dynamic_index_in_dim(by_chip, which, 1, keepdims=False)
        return lax.dot_general(
            part.reshape(half, block_width), head, NT, preferred_element_type=F32
        )

    other_core = lax.ppermute(hidden_terms(1 - core).astype(BF16), "dp", swap_core)
    terms = (hidden_terms(core) + other_core.astype(F32)).reshape(z_size, rows, -1)
    cut = rows // 2
    far = z_size // 2
    up = lax.ppermute(terms[far, :cut].astype(BF16), "dp", z_up)
    down = lax.ppermute(terms[far, cut:].astype(BF16), "dp", z_down)
    for step in range(far - 1, 0, -1):
        ahead, behind = terms[step], terms[z_size - step]
        if step == far - 1:
            ahead = jnp.concatenate([ahead[:cut] + up.astype(F32), ahead[cut:]], axis=0)
            behind = jnp.concatenate([behind[:cut], behind[cut:] + down.astype(F32)], axis=0)
        else:
            ahead = ahead + up.astype(F32)
            behind = behind + down.astype(F32)
        up = lax.ppermute(ahead.astype(BF16), "dp", z_up)
        down = lax.ppermute(behind.astype(BF16), "dp", z_down)
    row_terms = terms[0] + up.astype(F32) + down.astype(F32)
    parts = row_terms.reshape(rows, vocab_size, width).transpose(1, 0, 2).astype(BF16)
    parts = lax.all_to_all(parts, "vocab", split_axis=0, concat_axis=0, tiled=True)
    hidden_grad = jnp.sum(parts.astype(F32), axis=0)

    turned = lax.optimization_barrier(all_rows.T)
    head_grad = jnp.dot(turned, logit_grad, preferred_element_type=F32).astype(BF16)

    share_rows = half // dp_size
    kl_rows = lax.dynamic_slice_in_dim(token_kl, dp * share_rows, share_rows, 0)
    gap_rows = lax.dynamic_slice_in_dim(sampled_gap, dp * share_rows, share_rows, 0)
    return (head_grad, hidden_grad, kl_rows, gap_rows)


def solution(mesh):
    in_specs = (
        P("dp", ("sec", "vocab")),
        P("sec", ("dp", "vocab")),
        P(("sec", "dp"), "vocab"),
        P(),
        P(),
        P(),
    )
    out_specs = (
        P("sec", ("dp", "vocab")),
        P("dp", ("sec", "vocab")),
        P(("sec", "dp")),
        P(("sec", "dp")),
    )
    return jax.shard_map(
        on_device, mesh=mesh, in_specs=in_specs, out_specs=out_specs, check_vma=False
    )
```

```python
import functools

import jax
import jax.numpy as jnp
from jax import lax
from jax.experimental import pallas as pl
from jax.experimental.pallas import tpu as pltpu
from jax.sharding import PartitionSpec as P

F32 = jnp.float32
BF16 = jnp.bfloat16
NT = (((1,), (1,)), ((), ()))
TN = (((0,), (0,)), ((), ()))
INTERP = False
VMEM_LIMIT = 16 * 1024 * 1024


def call(kernel, flops, traffic, **spec):
    return pl.pallas_call(
        kernel,
        compiler_params=pltpu.CompilerParams(vmem_limit_bytes=VMEM_LIMIT),
        cost_estimate=pl.CostEstimate(flops=flops, bytes_accessed=traffic, transcendentals=0),
        interpret=INTERP,
        **spec,
    )


def whole(shape):
    return pl.BlockSpec(shape, lambda i: (0,) * len(shape))


BATCHES = ((0, 1, 7), (2, 6), (3, 4, 5))
PLACE = tuple(k for batch in BATCHES for k in batch)


def logits_kernel(parts, *refs):
    row_refs, (own_ref, partner_ref, mine_ref, theirs_ref) = refs[:-4], refs[-4:]
    blocks, at = [], 0
    for count in parts:
        blocks.append(jnp.concatenate([ref[...] for ref in row_refs[at : at + count]], axis=1))
        at += count
    rows = jnp.concatenate(blocks, axis=0)
    size = blocks[0].shape[0]
    cut = size // 2
    columns = own_ref.shape[1]
    for base, ref in ((0, own_ref), (columns, partner_ref)):
        for first in range(0, columns, 256):
            last = min(first + 256, columns)
            terms = jnp.dot(rows, ref[:, first:last], preferred_element_type=F32)
            for i in range(len(parts)):
                mine_ref[i, :, base + first : base + last] = terms[i * size : i * size + cut]
                theirs_ref[i, :, base + first : base + last] = terms[
                    i * size + cut : (i + 1) * size
                ]


def logits_of(blocks, own, partner):
    depth, columns = own.shape
    size = blocks[0][0].shape[0]
    flat = [piece for block in blocks for piece in block]
    count = len(blocks)
    out = jax.ShapeDtypeStruct((count, size // 2, 2 * columns), F32)
    return call(
        functools.partial(logits_kernel, tuple(len(block) for block in blocks)),
        4 * count * size * depth * columns,
        4 * depth * columns + 8 * count * size * columns,
        in_specs=in_vmem(len(flat) + 2),
        out_specs=in_vmem(2),
        out_shape=[out, out],
    )(*flat, own, partner)


def align_kernel(order_ref, token_ref, a_ref, b_ref, c_ref, d_ref, out_ref, choice_ref):
    lines = a_ref.shape[0]

    @pl.when(pl.program_id(0) == 0)
    def _():
        choice_ref[...] = jnp.where(order_ref[...] == token_ref[...], 1.0, 0.0).astype(BF16)

    total = None
    for i, ref in enumerate((a_ref, b_ref, c_ref, d_ref)):
        choice = choice_ref[:, i * lines : (i + 1) * lines]
        term = jnp.dot(choice, ref[...], preferred_element_type=F32)
        total = term if total is None else total + term
    out_ref[...] = total.astype(BF16)


def aligned(order, token, own, swapped):
    lines, columns = own[0].shape
    tiles = 6 if columns % 768 == 0 else 2
    tile = columns // tiles
    here = pl.BlockSpec((lines, tile), lambda i: (0, i))
    there = pl.BlockSpec((lines, tile), lambda i: (0, lax.rem(i + tiles // 2, tiles)))
    tokens = token.shape[0]
    return call(
        align_kernel,
        8 * tokens * lines * columns,
        12 * lines * columns,
        grid=(tiles,),
        in_specs=[whole(order.shape), whole(token.shape), here, here, there, there],
        out_specs=pl.BlockSpec((tokens, tile), lambda i: (0, i)),
        out_shape=jax.ShapeDtypeStruct((tokens, columns), BF16),
        scratch_shapes=[pltpu.VMEM((tokens, 4 * lines), BF16)],
    )(order, token, *own, *swapped)


def stats_kernel(z_ref, *refs):
    count = len(BATCHES)
    kept, received = refs[:count], refs[count : 2 * count]
    teacher_ref, target_ref, logits_ref, table_ref, columns_ref = refs[2 * count :]
    cut = kept[0].shape[1]
    lane = lax.broadcasted_iota(jnp.int32, (cut, 128), 1)

    def total(value):
        return jnp.sum(value, axis=1, keepdims=True)

    place = 0
    for b, batch in enumerate(BATCHES):
        for i, k in enumerate(batch):
            logits = kept[b][i] + received[b][i]
            logits_ref[place] = logits
            teacher = teacher_ref[place].astype(F32)[:cut]
            hit = lax.broadcasted_iota(jnp.int32, logits.shape, 1) == target_ref[place]
            top_s = jnp.max(logits, axis=1, keepdims=True)
            top_t = jnp.max(teacher, axis=1, keepdims=True)
            exp_s = jnp.exp(logits - top_s)
            columns = [
                top_s,
                total(exp_s),
                total(exp_s * (logits - teacher)),
                top_t,
                total(jnp.exp(teacher - top_t)),
                total(jnp.where(hit, logits, 0.0)),
                total(jnp.where(hit, teacher, 0.0)),
            ]
            table = jnp.zeros((cut, 128), F32)
            for j, column in enumerate(columns):
                table = jnp.where(lane == j, column, table)
            chip = lax.rem(z_ref[0] + k, len(PLACE))
            columns_ref[pl.ds(pl.multiple_of(chip * cut, 8), cut), :] = table
            place += 1
    lines = cut * len(PLACE)
    turned = columns_ref[...].T[:8, :lines]
    table_ref[...] = jnp.broadcast_to(turned[None], table_ref.shape)


def in_vmem(count):
    return [pl.BlockSpec(memory_space=pltpu.VMEM)] * count


def stats_of(z, kept, received, teacher, target, members):
    cut, columns = kept[0].shape[1:]
    chips = len(PLACE)
    lines = chips * cut
    padded = -(-lines // 128) * 128
    return call(
        stats_kernel,
        20 * lines * columns,
        14 * lines * columns,
        in_specs=[pl.BlockSpec(memory_space=pltpu.SMEM)] + in_vmem(2 * len(BATCHES) + 2),
        out_specs=in_vmem(2),
        out_shape=[
            jax.ShapeDtypeStruct((chips, cut, columns), F32),
            jax.ShapeDtypeStruct((members, 8, lines), F32),
        ],
        scratch_shapes=[pltpu.VMEM((padded, 128), F32)],
    )(z, *kept, *received, teacher, target)


def merged(table):
    max_s = jnp.max(table[:, 0], axis=0, keepdims=True)
    max_t = jnp.max(table[:, 3], axis=0, keepdims=True)
    scale_s = jnp.exp(table[:, 0] - max_s)
    scale_t = jnp.exp(table[:, 3] - max_t)

    def total(value):
        return jnp.sum(value, axis=0, keepdims=True)

    return [
        max_s,
        total(table[:, 1] * scale_s),
        total(table[:, 2] * scale_s),
        max_t,
        total(table[:, 4] * scale_t),
        total(table[:, 5]),
        total(table[:, 6]),
    ]


def merge_kernel(table_ref, out_ref):
    rows = merged(table_ref[...])
    table = jnp.concatenate(rows + [jnp.zeros_like(rows[0])], axis=0)
    out_ref[...] = jnp.broadcast_to(table[None], out_ref.shape)


def merge_of(table, members):
    lines = table.shape[2]
    return call(
        merge_kernel,
        16 * table.size,
        8 * table.size,
        out_shape=jax.ShapeDtypeStruct((members, 8, lines), F32),
    )(table)


def grad_kernel(place_ref, logits_ref, *refs):
    count = len(BATCHES)
    sent, received = refs[:count], refs[count : 2 * count]
    teacher_ref, table_ref, weight_ref, own_ref, partner_ref, rows_ref, columns_ref = refs[2 * count :]
    cut, columns = logits_ref.shape[1:]
    lines = cut * len(PLACE)
    padded = columns_ref.shape[1]
    members = table_ref.shape[0] // 2
    sec = place_ref[1]
    for i in range(2):
        which = sec if i == 0 else 1 - sec
        max_s, sum_s, cross, max_t, sum_t, pick_s, pick_t = merged(
            table_ref[pl.ds(which * members, members)]
        )
        student = max_s + jnp.log(sum_s)
        taught = max_t + jnp.log(sum_t)
        kl = cross / sum_s - student + taught
        gap = pick_s - student - (pick_t - taught)
        zero = jnp.zeros_like(kl)
        table = jnp.concatenate(
            [kl, gap, student, taught, weight_ref[i], zero, zero, zero], axis=0
        )
        rows_ref[which] = table
        table = jnp.concatenate([table, jnp.zeros((120, lines), F32)], axis=0)
        if padded > lines:
            table = jnp.concatenate([table, jnp.zeros((128, padded - lines), F32)], axis=1)
        columns_ref[i] = table.T

    def grad(logits, teacher, row):
        log_student = logits - row[:, 2:3]
        log_teacher = teacher - row[:, 3:4]
        return row[:, 4:5] * jnp.exp(log_student) * (log_student - log_teacher - row[:, 0:1])

    place = 0
    for b, batch in enumerate(BATCHES):
        for i, k in enumerate(batch):
            chip = lax.rem(place_ref[0] + k, len(PLACE))
            at = pl.ds(pl.multiple_of(chip * cut, 8), cut)
            teacher = teacher_ref[place].astype(F32)
            mine = grad(logits_ref[place], teacher[:cut], columns_ref[0, at, :])
            theirs = grad(sent[b][i] + received[b][i], teacher[cut:], columns_ref[1, at, :])
            both = jnp.concatenate([mine, theirs], axis=0).astype(BF16)
            own_ref[place] = both[:, : columns // 2]
            partner_ref[place] = both[:, columns // 2 :]
            place += 1


def grad_of(place, logits, sent, received, teacher, table, weight):
    chips, cut, columns = logits.shape
    lines = chips * cut
    padded = -(-lines // 128) * 128
    half = jax.ShapeDtypeStruct((chips, 2 * cut, columns // 2), BF16)
    return call(
        grad_kernel,
        20 * lines * columns,
        20 * lines * columns,
        in_specs=[pl.BlockSpec(memory_space=pltpu.SMEM)] + in_vmem(2 * len(BATCHES) + 4),
        out_specs=in_vmem(3),
        out_shape=[half, half, jax.ShapeDtypeStruct((2, 8, lines), F32)],
        scratch_shapes=[pltpu.VMEM((2, padded, 128), F32)],
    )(place, logits, *sent, *received, teacher, table, weight)


def terms_kernel(own_grad_ref, partner_grad_ref, own_ref, partner_ref, out_ref):
    members, width, _ = out_ref.shape
    group = members // 2
    for first in range(0, members, group):
        at = slice(first * width, (first + group) * width)
        terms = lax.dot_general(
            own_ref[at], own_grad_ref[...], NT, preferred_element_type=F32
        ) + lax.dot_general(
            partner_ref[at], partner_grad_ref[...], NT, preferred_element_type=F32
        )
        for i in range(group):
            out_ref[first + i] = terms[i * width : (i + 1) * width].astype(BF16)


def terms_of(own_grad, partner_grad, own, partner, members):
    chips, size, columns = own_grad.shape
    depth = own.shape[0]
    lines = chips * size
    return call(
        terms_kernel,
        4 * lines * columns * depth,
        4 * (lines + depth) * columns + 2 * lines * depth,
        in_specs=in_vmem(4),
        out_specs=in_vmem(1)[0],
        out_shape=jax.ShapeDtypeStruct((members, depth // members, lines), BF16),
    )(own_grad.reshape(lines, columns), partner_grad.reshape(lines, columns), own, partner)


def sum_kernel(place_ref, parts_ref, out_ref):
    size = out_ref.shape[1]
    total = None
    for member in range(parts_ref.shape[0]):
        term = parts_ref[member].astype(F32)
        total = term if total is None else total + term
    total = total.T.astype(BF16)
    for i, k in enumerate(PLACE):
        chip = lax.rem(place_ref[0] + k, len(PLACE))
        out_ref[chip] = total[i * size : (i + 1) * size]


def sum_of(place, parts):
    members, width, lines = parts.shape
    chips = len(PLACE)
    return call(
        sum_kernel,
        parts.size,
        2 * parts.size,
        in_specs=[pl.BlockSpec(memory_space=pltpu.SMEM)] + in_vmem(1),
        out_specs=in_vmem(1)[0],
        out_shape=jax.ShapeDtypeStruct((chips, lines // chips, width), BF16),
    )(place, parts)


def head_grad_kernel(a_rows_ref, b_rows_ref, a_grad_ref, b_grad_ref, out_ref):
    terms = lax.dot_general(a_rows_ref[...], a_grad_ref[...], TN, preferred_element_type=F32)
    terms += lax.dot_general(b_rows_ref[...], b_grad_ref[...], TN, preferred_element_type=F32)
    out_ref[...] = terms.astype(BF16)


def head_grad_of(a_rows, b_rows, a_grad, b_grad):
    lines, depth = a_rows.shape
    columns = a_grad.shape[-1]
    tile = min(256, depth)
    rows = pl.BlockSpec((lines, tile), lambda i: (0, i))
    return call(
        head_grad_kernel,
        4 * lines * depth * columns,
        4 * (lines * depth + lines * columns) + 2 * depth * columns,
        grid=(depth // tile,),
        in_specs=[rows, rows, whole((lines, columns)), whole((lines, columns))],
        out_specs=pl.BlockSpec((tile, columns), lambda i: (i, 0)),
        out_shape=jax.ShapeDtypeStruct((depth, columns), BF16),
    )(a_rows, b_rows, a_grad.reshape(lines, columns), b_grad.reshape(lines, columns))


def exchange(copies, axis, groups=None):
    return lax.all_to_all(
        copies, axis, split_axis=0, concat_axis=0, tiled=True, axis_index_groups=groups
    )


def on_device(hidden, head, teacher_logits, loss_mask, token_ids, row_order):
    dp_size = lax.axis_size("dp")
    vocab_size = lax.axis_size("vocab")
    z_size = dp_size // 2
    far = z_size // 2
    sec = lax.axis_index("sec")
    dp = lax.axis_index("dp")
    vocab = lax.axis_index("vocab")
    z, core = dp // 2, dp % 2
    block_width = head.shape[1]
    rows, width = hidden.shape
    cut = rows // 2
    lines = z_size * cut
    teacher_rows = teacher_logits.shape[0]
    swap_sec = [(0, 1), (1, 0)]
    swap_core = [(i, i ^ 1) for i in range(dp_size)]
    along = [[2 * i + c for i in range(z_size)] for c in range(2)]

    def shift(by):
        return [(i, (i + 2 * by) % dp_size) for i in range(dp_size)]

    def to_partner(value):
        return lax.ppermute(value, "dp", swap_core)

    head_partner = to_partner(head)
    arranged = jnp.where(sec == 0, hidden, jnp.concatenate([hidden[cut:], hidden[:cut]], axis=0))
    copies = jnp.broadcast_to(arranged[None], (vocab_size, rows, width))
    features = exchange(copies, "vocab").transpose(1, 0, 2).reshape(rows, vocab_size * width)

    tiles = teacher_logits.reshape(teacher_rows, 2, vocab_size, block_width)
    tiles = jnp.where(core == 0, tiles, jnp.concatenate([tiles[:, 1:], tiles[:, :1]], axis=1))
    tiles, features = lax.optimization_barrier((tiles, features))
    tiles = lax.all_to_all(tiles, "vocab", split_axis=2, concat_axis=1, tiled=True)
    tiles = tiles.reshape(teacher_rows, z_size, 2 * block_width)

    blocks = {0: [features]}
    kept, sent, received = [], [], []

    def take(batch):
        mine, theirs = logits_of([blocks[k] for k in batch], head, head_partner)
        kept.append(mine)
        sent.append(theirs)
        received.append(lax.ppermute(theirs, "sec", swap_sec))

    up, down = features, features
    middle = features.shape[1] // 2
    for step in range(1, far):
        up = lax.ppermute(up, "dp", shift(1))
        down = lax.ppermute(down, "dp", shift(-1))
        blocks[step], blocks[z_size - step] = [down], [up]
        if step == 2:
            up, down, kept[0] = lax.optimization_barrier((up, down, kept[0]))
        if step == 3:
            up, down, kept[1], received[0] = lax.optimization_barrier(
                (up, down, kept[1], received[0])
            )
        if step < far - 1:
            take(BATCHES[step - 1])
    blocks[far] = [
        lax.ppermute(up[:, :middle], "dp", shift(1)),
        lax.ppermute(down[:, middle:], "dp", shift(-1)),
    ]
    blocks[far], tiles, received[1] = lax.optimization_barrier((blocks[far], tiles, received[1]))
    teacher = lax.all_to_all(
        tiles, "dp", split_axis=1, concat_axis=0, tiled=True, axis_index_groups=along
    ).reshape(lines, 2 * block_width)
    take(BATCHES[2])
    teacher, received[2] = lax.optimization_barrier((teacher, received[2]))
    teacher_across = lax.ppermute(teacher, "sec", swap_sec)

    chips = (z + jnp.array(PLACE, jnp.int32)) % z_size
    line = jnp.arange(cut, dtype=jnp.int32)

    def tokens_at(chip, which):
        return (((chip * 2 + core) * rows + which * cut)[:, None] + line).astype(jnp.int32)

    token = jnp.concatenate([tokens_at(chips, sec), tokens_at(chips, 1 - sec)], axis=1)
    by_device = row_order.reshape(2, z_size, 2, teacher_rows)

    def order_of(section, parity):
        part = lax.dynamic_index_in_dim(by_device, section, 0, keepdims=False)
        return lax.dynamic_index_in_dim(part, parity, 1, keepdims=False).reshape(-1)

    order = jnp.concatenate(
        [order_of(a, c) for c in (core, 1 - core) for a in (sec, 1 - sec)]
    )
    taught = aligned(
        order[None, :],
        token.reshape(-1, 1),
        (teacher, teacher_across),
        (to_partner(teacher), to_partner(teacher_across)),
    ).reshape(z_size, rows, 2 * block_width)

    ids = jnp.take(token_ids, tokens_at(chips, sec))
    from_own = ids - ((2 * z + core) * vocab_size + vocab) * block_width
    from_partner = ids - ((2 * z + 1 - core) * vocab_size + vocab) * block_width

    def inside(value):
        return (value >= 0) & (value < block_width)

    target = jnp.where(
        inside(from_own), from_own, jnp.where(inside(from_partner), from_partner + block_width, -1)
    )
    place = jnp.stack([z, sec]).astype(jnp.int32)
    logits, table = stats_of(place, kept, received, taught, target[:, :, None], z_size)
    table = exchange(merge_of(exchange(table, "dp", along), 2 * vocab_size), ("sec", "vocab"))

    held, _ = lax.optimization_barrier((tuple(kept), teacher_across))
    returned = [lax.ppermute(part, "sec", swap_sec) for part in held]

    every = jnp.arange(z_size, dtype=jnp.int32)
    weight = jnp.stack(
        [jnp.take(loss_mask, tokens_at(every, a)).reshape(1, lines) for a in (sec, 1 - sec)]
    ).astype(F32)
    own_grad, partner_grad, per_row = grad_of(
        place, logits, sent, returned, taught, table, weight
    )

    terms = terms_of(own_grad, partner_grad, head, head_partner, vocab_size)
    by_chip = sum_of(place, exchange(terms, "vocab"))
    own_rows = jnp.concatenate([jnp.concatenate(blocks[k], axis=1) for k in PLACE], axis=0)
    head_grad = head_grad_of(
        own_rows, to_partner(own_rows), own_grad, to_partner(partner_grad)
    )

    by_chip, head_grad = lax.optimization_barrier((by_chip, head_grad))
    hidden_grad = jnp.sum(exchange(by_chip, "dp", along).astype(F32), axis=0)
    hidden_grad = jnp.where(
        sec == 0, hidden_grad, jnp.concatenate([hidden_grad[cut:], hidden_grad[:cut]], axis=0)
    )

    other_rows = to_partner(per_row)
    per_row = jnp.where(z % 2 == core, per_row, other_rows)
    per_row = lax.dynamic_index_in_dim(per_row, core, 0, keepdims=False)
    per_row = lax.dynamic_slice_in_dim(per_row, (sec * (z_size // 2) + z // 2) * cut, cut, 1)
    return (head_grad, hidden_grad, per_row[0], per_row[1])


def solution(mesh):
    in_specs = (
        P("dp", ("sec", "vocab")),
        P("sec", ("dp", "vocab")),
        P(("sec", "dp"), "vocab"),
        P(),
        P(),
        P(),
    )
    out_specs = (
        P("sec", ("dp", "vocab")),
        P("dp", ("sec", "vocab")),
        P(("sec", "dp")),
        P(("sec", "dp")),
    )
    return jax.shard_map(
        on_device, mesh=mesh, in_specs=in_specs, out_specs=out_specs, check_vma=False
    )
```

```python
import functools

import jax
import jax.numpy as jnp
from jax import lax
from jax.experimental import pallas as pl
from jax.experimental.pallas import tpu as pltpu
from jax.sharding import PartitionSpec as P

F32 = jnp.float32
BF16 = jnp.bfloat16
NT = (((1,), (1,)), ((), ()))
TN = (((0,), (0,)), ((), ()))
INTERP = False
VMEM_LIMIT = 16 * 1024 * 1024


def call(kernel, flops, traffic, **spec):
    return pl.pallas_call(
        kernel,
        compiler_params=pltpu.CompilerParams(vmem_limit_bytes=VMEM_LIMIT),
        cost_estimate=pl.CostEstimate(flops=flops, bytes_accessed=traffic, transcendentals=0),
        interpret=INTERP,
        **spec,
    )


def whole(shape):
    return pl.BlockSpec(shape, lambda i: (0,) * len(shape))


BATCHES = ((0, 1, 7), (2, 6), (3, 4, 5))
PLACE = tuple(k for batch in BATCHES for k in batch)


def logits_kernel(parts, *refs):
    row_refs, (own_ref, partner_ref, mine_ref, theirs_ref) = refs[:-4], refs[-4:]
    blocks, at = [], 0
    for count in parts:
        blocks.append(jnp.concatenate([ref[...] for ref in row_refs[at : at + count]], axis=1))
        at += count
    rows = jnp.concatenate(blocks, axis=0)
    size = blocks[0].shape[0]
    cut = size // 2
    columns = own_ref.shape[1]
    for base, ref in ((0, own_ref), (columns, partner_ref)):
        for first in range(0, columns, 256):
            last = min(first + 256, columns)
            terms = jnp.dot(rows, ref[:, first:last], preferred_element_type=F32)
            for i in range(len(parts)):
                mine_ref[i, :, base + first : base + last] = terms[i * size : i * size + cut]
                theirs_ref[i, :, base + first : base + last] = terms[
                    i * size + cut : (i + 1) * size
                ]


def logits_of(blocks, own, partner):
    depth, columns = own.shape
    size = blocks[0][0].shape[0]
    flat = [piece for block in blocks for piece in block]
    count = len(blocks)
    out = jax.ShapeDtypeStruct((count, size // 2, 2 * columns), F32)
    return call(
        functools.partial(logits_kernel, tuple(len(block) for block in blocks)),
        4 * count * size * depth * columns,
        4 * depth * columns + 8 * count * size * columns,
        in_specs=in_vmem(len(flat) + 2),
        out_specs=in_vmem(2),
        out_shape=[out, out],
    )(*flat, own, partner)


def align_kernel(order_ref, token_ref, a_ref, b_ref, c_ref, d_ref, out_ref, choice_ref):
    lines = a_ref.shape[0]

    @pl.when(pl.program_id(0) == 0)
    def _():
        choice_ref[...] = jnp.where(order_ref[...] == token_ref[...], 1.0, 0.0).astype(BF16)

    total = None
    for i, ref in enumerate((a_ref, b_ref, c_ref, d_ref)):
        choice = choice_ref[:, i * lines : (i + 1) * lines]
        term = jnp.dot(choice, ref[...], preferred_element_type=F32)
        total = term if total is None else total + term
    out_ref[...] = total.astype(BF16)


def aligned(order, token, own, swapped):
    lines, columns = own[0].shape
    tiles = 6 if columns % 768 == 0 else 2
    tile = columns // tiles
    here = pl.BlockSpec((lines, tile), lambda i: (0, i))
    there = pl.BlockSpec((lines, tile), lambda i: (0, lax.rem(i + tiles // 2, tiles)))
    tokens = token.shape[0]
    return call(
        align_kernel,
        8 * tokens * lines * columns,
        12 * lines * columns,
        grid=(tiles,),
        in_specs=[whole(order.shape), whole(token.shape), here, here, there, there],
        out_specs=pl.BlockSpec((tokens, tile), lambda i: (0, i)),
        out_shape=jax.ShapeDtypeStruct((tokens, columns), BF16),
        scratch_shapes=[pltpu.VMEM((tokens, 4 * lines), BF16)],
    )(order, token, *own, *swapped)


def stats_kernel(z_ref, *refs):
    count = len(BATCHES)
    kept, received = refs[:count], refs[count : 2 * count]
    teacher_ref, target_ref, logits_ref, table_ref, columns_ref = refs[2 * count :]
    cut = kept[0].shape[1]
    lane = lax.broadcasted_iota(jnp.int32, (cut, 128), 1)

    def total(value):
        return jnp.sum(value, axis=1, keepdims=True)

    place = 0
    for b, batch in enumerate(BATCHES):
        for i, k in enumerate(batch):
            logits = kept[b][i] + received[b][i]
            logits_ref[place] = logits
            teacher = teacher_ref[place].astype(F32)[:cut]
            hit = lax.broadcasted_iota(jnp.int32, logits.shape, 1) == target_ref[place]
            top_s = jnp.max(logits, axis=1, keepdims=True)
            top_t = jnp.max(teacher, axis=1, keepdims=True)
            exp_s = jnp.exp(logits - top_s)
            columns = [
                top_s,
                total(exp_s),
                total(exp_s * (logits - teacher)),
                top_t,
                total(jnp.exp(teacher - top_t)),
                total(jnp.where(hit, logits, 0.0)),
                total(jnp.where(hit, teacher, 0.0)),
            ]
            table = jnp.zeros((cut, 128), F32)
            for j, column in enumerate(columns):
                table = jnp.where(lane == j, column, table)
            chip = lax.rem(z_ref[0] + k, len(PLACE))
            columns_ref[pl.ds(pl.multiple_of(chip * cut, 8), cut), :] = table
            place += 1
    lines = cut * len(PLACE)
    turned = columns_ref[...].T[:8, :lines]
    table_ref[...] = jnp.broadcast_to(turned[None], table_ref.shape)


def in_vmem(count):
    return [pl.BlockSpec(memory_space=pltpu.VMEM)] * count


def stats_of(z, kept, received, teacher, target, members):
    cut, columns = kept[0].shape[1:]
    chips = len(PLACE)
    lines = chips * cut
    padded = -(-lines // 128) * 128
    return call(
        stats_kernel,
        20 * lines * columns,
        14 * lines * columns,
        in_specs=[pl.BlockSpec(memory_space=pltpu.SMEM)] + in_vmem(2 * len(BATCHES) + 2),
        out_specs=in_vmem(2),
        out_shape=[
            jax.ShapeDtypeStruct((chips, cut, columns), F32),
            jax.ShapeDtypeStruct((members, 8, lines), F32),
        ],
        scratch_shapes=[pltpu.VMEM((padded, 128), F32)],
    )(z, *kept, *received, teacher, target)


def merged(table):
    max_s = jnp.max(table[:, 0], axis=0, keepdims=True)
    max_t = jnp.max(table[:, 3], axis=0, keepdims=True)
    scale_s = jnp.exp(table[:, 0] - max_s)
    scale_t = jnp.exp(table[:, 3] - max_t)

    def total(value):
        return jnp.sum(value, axis=0, keepdims=True)

    return [
        max_s,
        total(table[:, 1] * scale_s),
        total(table[:, 2] * scale_s),
        max_t,
        total(table[:, 4] * scale_t),
        total(table[:, 5]),
        total(table[:, 6]),
    ]


def merge_kernel(table_ref, out_ref):
    rows = merged(table_ref[...])
    table = jnp.concatenate(rows + [jnp.zeros_like(rows[0])], axis=0)
    out_ref[...] = jnp.broadcast_to(table[None], out_ref.shape)


def merge_of(table, members):
    lines = table.shape[2]
    return call(
        merge_kernel,
        16 * table.size,
        8 * table.size,
        out_shape=jax.ShapeDtypeStruct((members, 8, lines), F32),
    )(table)


def grad_kernel(place_ref, logits_ref, *refs):
    count = len(BATCHES)
    sent, received = refs[:count], refs[count : 2 * count]
    teacher_ref, table_ref, weight_ref, own_ref, partner_ref, rows_ref, columns_ref = refs[2 * count :]
    cut, columns = logits_ref.shape[1:]
    lines = cut * len(PLACE)
    padded = columns_ref.shape[1]
    members = table_ref.shape[0] // 2
    sec = place_ref[1]
    for i in range(2):
        which = sec if i == 0 else 1 - sec
        max_s, sum_s, cross, max_t, sum_t, pick_s, pick_t = merged(
            table_ref[pl.ds(which * members, members)]
        )
        student = max_s + jnp.log(sum_s)
        taught = max_t + jnp.log(sum_t)
        kl = cross / sum_s - student + taught
        gap = pick_s - student - (pick_t - taught)
        zero = jnp.zeros_like(kl)
        table = jnp.concatenate(
            [kl, gap, student, taught, weight_ref[i], zero, zero, zero], axis=0
        )
        rows_ref[which] = table
        table = jnp.concatenate([table, jnp.zeros((120, lines), F32)], axis=0)
        if padded > lines:
            table = jnp.concatenate([table, jnp.zeros((128, padded - lines), F32)], axis=1)
        columns_ref[i] = table.T

    def grad(logits, teacher, row):
        log_student = logits - row[:, 2:3]
        log_teacher = teacher - row[:, 3:4]
        return row[:, 4:5] * jnp.exp(log_student) * (log_student - log_teacher - row[:, 0:1])

    place = 0
    for b, batch in enumerate(BATCHES):
        for i, k in enumerate(batch):
            chip = lax.rem(place_ref[0] + k, len(PLACE))
            at = pl.ds(pl.multiple_of(chip * cut, 8), cut)
            teacher = teacher_ref[place].astype(F32)
            mine = grad(logits_ref[place], teacher[:cut], columns_ref[0, at, :])
            theirs = grad(sent[b][i] + received[b][i], teacher[cut:], columns_ref[1, at, :])
            both = jnp.concatenate([mine, theirs], axis=0).astype(BF16)
            own_ref[place] = both[:, : columns // 2]
            partner_ref[place] = both[:, columns // 2 :]
            place += 1


def grad_of(place, logits, sent, received, teacher, table, weight):
    chips, cut, columns = logits.shape
    lines = chips * cut
    padded = -(-lines // 128) * 128
    half = jax.ShapeDtypeStruct((chips, 2 * cut, columns // 2), BF16)
    return call(
        grad_kernel,
        20 * lines * columns,
        20 * lines * columns,
        in_specs=[pl.BlockSpec(memory_space=pltpu.SMEM)] + in_vmem(2 * len(BATCHES) + 4),
        out_specs=in_vmem(3),
        out_shape=[half, half, jax.ShapeDtypeStruct((2, 8, lines), F32)],
        scratch_shapes=[pltpu.VMEM((2, padded, 128), F32)],
    )(place, logits, *sent, *received, teacher, table, weight)


def terms_kernel(own_grad_ref, partner_grad_ref, own_ref, partner_ref, out_ref):
    terms = lax.dot_general(own_ref[...], own_grad_ref[...], NT, preferred_element_type=F32)
    terms += lax.dot_general(
        partner_ref[...], partner_grad_ref[...], NT, preferred_element_type=F32
    )
    out_ref[0] = terms.astype(BF16)


def terms_of(own_grad, partner_grad, own, partner, members):
    chips, size, columns = own_grad.shape
    depth = own.shape[0]
    lines = chips * size
    width = depth // members
    weights = pl.BlockSpec((width, columns), lambda i: (i, 0))
    return call(
        terms_kernel,
        4 * lines * columns * depth,
        4 * (lines + depth) * columns + 2 * lines * depth,
        grid=(members,),
        in_specs=[whole((lines, columns))] * 2 + [weights] * 2,
        out_specs=pl.BlockSpec((1, width, lines), lambda i: (i, 0, 0)),
        out_shape=jax.ShapeDtypeStruct((members, width, lines), BF16),
    )(own_grad.reshape(lines, columns), partner_grad.reshape(lines, columns), own, partner)


def sum_kernel(place_ref, parts_ref, out_ref):
    size = out_ref.shape[1]
    total = None
    for member in range(parts_ref.shape[0]):
        term = parts_ref[member].astype(F32)
        total = term if total is None else total + term
    total = total.T.astype(BF16)
    for i, k in enumerate(PLACE):
        chip = lax.rem(place_ref[0] + k, len(PLACE))
        out_ref[chip] = total[i * size : (i + 1) * size]


def sum_of(place, parts):
    members, width, lines = parts.shape
    chips = len(PLACE)
    return call(
        sum_kernel,
        parts.size,
        2 * parts.size,
        in_specs=[pl.BlockSpec(memory_space=pltpu.SMEM)] + in_vmem(1),
        out_specs=in_vmem(1)[0],
        out_shape=jax.ShapeDtypeStruct((chips, lines // chips, width), BF16),
    )(place, parts)


def head_grad_kernel(a_rows_ref, b_rows_ref, a_grad_ref, b_grad_ref, out_ref):
    terms = lax.dot_general(a_rows_ref[...], a_grad_ref[...], TN, preferred_element_type=F32)
    terms += lax.dot_general(b_rows_ref[...], b_grad_ref[...], TN, preferred_element_type=F32)
    out_ref[...] = terms.astype(BF16)


def head_grad_of(a_rows, b_rows, a_grad, b_grad):
    lines, depth = a_rows.shape
    columns = a_grad.shape[-1]
    tile = min(256, depth)
    rows = pl.BlockSpec((lines, tile), lambda i: (0, i))
    return call(
        head_grad_kernel,
        4 * lines * depth * columns,
        4 * (lines * depth + lines * columns) + 2 * depth * columns,
        grid=(depth // tile,),
        in_specs=[rows, rows, whole((lines, columns)), whole((lines, columns))],
        out_specs=pl.BlockSpec((tile, columns), lambda i: (i, 0)),
        out_shape=jax.ShapeDtypeStruct((depth, columns), BF16),
    )(a_rows, b_rows, a_grad.reshape(lines, columns), b_grad.reshape(lines, columns))


def exchange(copies, axis, groups=None):
    return lax.all_to_all(
        copies, axis, split_axis=0, concat_axis=0, tiled=True, axis_index_groups=groups
    )


def on_device(hidden, head, teacher_logits, loss_mask, token_ids, row_order):
    dp_size = lax.axis_size("dp")
    vocab_size = lax.axis_size("vocab")
    z_size = dp_size // 2
    far = z_size // 2
    sec = lax.axis_index("sec")
    dp = lax.axis_index("dp")
    vocab = lax.axis_index("vocab")
    z, core = dp // 2, dp % 2
    block_width = head.shape[1]
    rows, width = hidden.shape
    cut = rows // 2
    lines = z_size * cut
    teacher_rows = teacher_logits.shape[0]
    swap_sec = [(0, 1), (1, 0)]
    swap_core = [(i, i ^ 1) for i in range(dp_size)]
    along = [[2 * i + c for i in range(z_size)] for c in range(2)]

    def shift(by):
        return [(i, (i + 2 * by) % dp_size) for i in range(dp_size)]

    def to_partner(value):
        return lax.ppermute(value, "dp", swap_core)

    head_partner = to_partner(head)
    arranged = jnp.where(sec == 0, hidden, jnp.concatenate([hidden[cut:], hidden[:cut]], axis=0))
    copies = jnp.broadcast_to(arranged[None], (vocab_size, rows, width))
    features = exchange(copies, "vocab").transpose(1, 0, 2).reshape(rows, vocab_size * width)

    tiles = teacher_logits.reshape(teacher_rows, 2, vocab_size, block_width)
    tiles = jnp.where(core == 0, tiles, jnp.concatenate([tiles[:, 1:], tiles[:, :1]], axis=1))
    tiles, features = lax.optimization_barrier((tiles, features))
    tiles = lax.all_to_all(tiles, "vocab", split_axis=2, concat_axis=1, tiled=True)
    tiles = tiles.reshape(teacher_rows, z_size, 2 * block_width)

    blocks = {0: [features]}
    kept, sent, received = [], [], []

    def take(batch, *before):
        mine, theirs = logits_of([blocks[k] for k in batch], head, head_partner)
        kept.append(mine)
        sent.append(theirs)
        if before:
            theirs = lax.optimization_barrier((theirs,) + before)[0]
        received.append(lax.ppermute(theirs, "sec", swap_sec))

    up, down = features, features
    middle = features.shape[1] // 2
    for step in range(1, far):
        up = lax.ppermute(up, "dp", shift(1))
        down = lax.ppermute(down, "dp", shift(-1))
        blocks[step], blocks[z_size - step] = [down], [up]
        if step == 1:
            up, down, tiles = lax.optimization_barrier((up, down, tiles))
        if step == 2:
            up, down, kept[0] = lax.optimization_barrier((up, down, kept[0]))
        if step < far - 1:
            take(BATCHES[step - 1])
    blocks[far] = [
        lax.ppermute(up[:, :middle], "dp", shift(1)),
        lax.ppermute(down[:, middle:], "dp", shift(-1)),
    ]
    blocks[far], received[0] = lax.optimization_barrier((blocks[far], received[0]))
    take(BATCHES[2])
    tiles = lax.optimization_barrier((tiles, kept[2], received[1]))[0]
    teacher = lax.all_to_all(
        tiles, "dp", split_axis=1, concat_axis=0, tiled=True, axis_index_groups=along
    ).reshape(lines, 2 * block_width)
    teacher = lax.optimization_barrier((teacher, received[2]))[0]
    teacher_across = lax.ppermute(teacher, "sec", swap_sec)

    chips = (z + jnp.array(PLACE, jnp.int32)) % z_size
    line = jnp.arange(cut, dtype=jnp.int32)

    def tokens_at(chip, which):
        return (((chip * 2 + core) * rows + which * cut)[:, None] + line).astype(jnp.int32)

    token = jnp.concatenate([tokens_at(chips, sec), tokens_at(chips, 1 - sec)], axis=1)
    by_device = row_order.reshape(2, z_size, 2, teacher_rows)

    def order_of(section, parity):
        part = lax.dynamic_index_in_dim(by_device, section, 0, keepdims=False)
        return lax.dynamic_index_in_dim(part, parity, 1, keepdims=False).reshape(-1)

    order = jnp.concatenate(
        [order_of(a, c) for c in (core, 1 - core) for a in (sec, 1 - sec)]
    )
    taught = aligned(
        order[None, :],
        token.reshape(-1, 1),
        (teacher, teacher_across),
        (to_partner(teacher), to_partner(teacher_across)),
    ).reshape(z_size, rows, 2 * block_width)

    ids = jnp.take(token_ids, tokens_at(chips, sec))
    from_own = ids - ((2 * z + core) * vocab_size + vocab) * block_width
    from_partner = ids - ((2 * z + 1 - core) * vocab_size + vocab) * block_width

    def inside(value):
        return (value >= 0) & (value < block_width)

    target = jnp.where(
        inside(from_own), from_own, jnp.where(inside(from_partner), from_partner + block_width, -1)
    )
    place = jnp.stack([z, sec]).astype(jnp.int32)
    logits, table = stats_of(place, kept, received, taught, target[:, :, None], z_size)
    table = exchange(merge_of(exchange(table, "dp", along), 2 * vocab_size), ("sec", "vocab"))

    held = lax.optimization_barrier((tuple(kept), received[2], teacher_across))[0]
    returned = [lax.ppermute(part, "sec", swap_sec) for part in held]

    every = jnp.arange(z_size, dtype=jnp.int32)
    weight = jnp.stack(
        [jnp.take(loss_mask, tokens_at(every, a)).reshape(1, lines) for a in (sec, 1 - sec)]
    ).astype(F32)
    own_grad, partner_grad, per_row = grad_of(
        place, logits, sent, returned, taught, table, weight
    )

    terms = terms_of(own_grad, partner_grad, head, head_partner, vocab_size)
    by_chip = sum_of(place, exchange(terms, "vocab"))
    own_rows = jnp.concatenate([jnp.concatenate(blocks[k], axis=1) for k in PLACE], axis=0)
    head_grad = head_grad_of(
        own_rows, to_partner(own_rows), own_grad, to_partner(partner_grad)
    )

    by_chip, head_grad = lax.optimization_barrier((by_chip, head_grad))
    hidden_grad = jnp.sum(exchange(by_chip, "dp", along).astype(F32), axis=0)
    hidden_grad = jnp.where(
        sec == 0, hidden_grad, jnp.concatenate([hidden_grad[cut:], hidden_grad[:cut]], axis=0)
    )

    other_rows = to_partner(per_row)
    per_row = jnp.where(z % 2 == core, per_row, other_rows)
    per_row = lax.dynamic_index_in_dim(per_row, core, 0, keepdims=False)
    per_row = lax.dynamic_slice_in_dim(per_row, (sec * (z_size // 2) + z // 2) * cut, cut, 1)
    return (head_grad, hidden_grad, per_row[0], per_row[1])


def solution(mesh):
    in_specs = (
        P("dp", ("sec", "vocab")),
        P("sec", ("dp", "vocab")),
        P(("sec", "dp"), "vocab"),
        P(),
        P(),
        P(),
    )
    out_specs = (
        P("sec", ("dp", "vocab")),
        P("dp", ("sec", "vocab")),
        P(("sec", "dp")),
        P(("sec", "dp")),
    )
    return jax.shard_map(
        on_device, mesh=mesh, in_specs=in_specs, out_specs=out_specs, check_vma=False
    )
```

```python
import functools

import jax
import jax.numpy as jnp
from jax import lax
from jax.experimental import pallas as pl
from jax.experimental.pallas import tpu as pltpu
from jax.sharding import PartitionSpec as P

F32 = jnp.float32
BF16 = jnp.bfloat16
NT = (((1,), (1,)), ((), ()))
TN = (((0,), (0,)), ((), ()))
INTERP = False
VMEM_LIMIT = 16 * 1024 * 1024


def call(kernel, flops, traffic, **spec):
    return pl.pallas_call(
        kernel,
        compiler_params=pltpu.CompilerParams(vmem_limit_bytes=VMEM_LIMIT),
        cost_estimate=pl.CostEstimate(flops=flops, bytes_accessed=traffic, transcendentals=0),
        interpret=INTERP,
        **spec,
    )


def whole(shape):
    return pl.BlockSpec(shape, lambda i: (0,) * len(shape))


BATCHES = ((0, 1, 7), (2, 6), (3, 4, 5))
PLACE = tuple(k for batch in BATCHES for k in batch)


def logits_kernel(parts, *refs):
    row_refs, (own_ref, partner_ref, mine_ref, theirs_ref) = refs[:-4], refs[-4:]
    blocks, at = [], 0
    for count in parts:
        blocks.append(jnp.concatenate([ref[...] for ref in row_refs[at : at + count]], axis=1))
        at += count
    rows = jnp.concatenate(blocks, axis=0)
    size = blocks[0].shape[0]
    cut = size // 2
    columns = own_ref.shape[1]
    for base, ref in ((0, own_ref), (columns, partner_ref)):
        for first in range(0, columns, 256):
            last = min(first + 256, columns)
            terms = jnp.dot(rows, ref[:, first:last], preferred_element_type=F32)
            for i in range(len(parts)):
                mine_ref[i, :, base + first : base + last] = terms[i * size : i * size + cut]
                theirs_ref[i, :, base + first : base + last] = terms[
                    i * size + cut : (i + 1) * size
                ]


def logits_of(blocks, own, partner):
    depth, columns = own.shape
    size = blocks[0][0].shape[0]
    flat = [piece for block in blocks for piece in block]
    count = len(blocks)
    out = jax.ShapeDtypeStruct((count, size // 2, 2 * columns), F32)
    return call(
        functools.partial(logits_kernel, tuple(len(block) for block in blocks)),
        4 * count * size * depth * columns,
        4 * depth * columns + 8 * count * size * columns,
        in_specs=in_vmem(len(flat) + 2),
        out_specs=in_vmem(2),
        out_shape=[out, out],
    )(*flat, own, partner)


def align_kernel(order_ref, token_ref, a_ref, b_ref, c_ref, d_ref, out_ref, choice_ref):
    lines = a_ref.shape[0]

    @pl.when(pl.program_id(0) == 0)
    def _():
        choice_ref[...] = jnp.where(order_ref[...] == token_ref[...], 1.0, 0.0).astype(BF16)

    total = None
    for i, ref in enumerate((a_ref, b_ref, c_ref, d_ref)):
        choice = choice_ref[:, i * lines : (i + 1) * lines]
        term = jnp.dot(choice, ref[...], preferred_element_type=F32)
        total = term if total is None else total + term
    out_ref[...] = total.astype(BF16)


def aligned(order, token, own, swapped):
    lines, columns = own[0].shape
    tiles = 6 if columns % 768 == 0 else 2
    tile = columns // tiles
    here = pl.BlockSpec((lines, tile), lambda i: (0, i))
    there = pl.BlockSpec((lines, tile), lambda i: (0, lax.rem(i + tiles // 2, tiles)))
    tokens = token.shape[0]
    return call(
        align_kernel,
        8 * tokens * lines * columns,
        12 * lines * columns,
        grid=(tiles,),
        in_specs=[whole(order.shape), whole(token.shape), here, here, there, there],
        out_specs=pl.BlockSpec((tokens, tile), lambda i: (0, i)),
        out_shape=jax.ShapeDtypeStruct((tokens, columns), BF16),
        scratch_shapes=[pltpu.VMEM((tokens, 4 * lines), BF16)],
    )(order, token, *own, *swapped)


def stats_kernel(z_ref, *refs):
    count = len(BATCHES)
    kept, received = refs[:count], refs[count : 2 * count]
    teacher_ref, target_ref, logits_ref, table_ref, columns_ref = refs[2 * count :]
    cut = kept[0].shape[1]
    lane = lax.broadcasted_iota(jnp.int32, (cut, 128), 1)

    def total(value):
        return jnp.sum(value, axis=1, keepdims=True)

    place = 0
    for b, batch in enumerate(BATCHES):
        for i, k in enumerate(batch):
            logits = kept[b][i] + received[b][i]
            logits_ref[place] = logits
            teacher = teacher_ref[place].astype(F32)[:cut]
            hit = lax.broadcasted_iota(jnp.int32, logits.shape, 1) == target_ref[place]
            top_s = jnp.max(logits, axis=1, keepdims=True)
            top_t = jnp.max(teacher, axis=1, keepdims=True)
            exp_s = jnp.exp(logits - top_s)
            columns = [
                top_s,
                total(exp_s),
                total(exp_s * (logits - teacher)),
                top_t,
                total(jnp.exp(teacher - top_t)),
                total(jnp.where(hit, logits, 0.0)),
                total(jnp.where(hit, teacher, 0.0)),
            ]
            table = jnp.zeros((cut, 128), F32)
            for j, column in enumerate(columns):
                table = jnp.where(lane == j, column, table)
            chip = lax.rem(z_ref[0] + k, len(PLACE))
            columns_ref[pl.ds(pl.multiple_of(chip * cut, 8), cut), :] = table
            place += 1
    lines = cut * len(PLACE)
    turned = columns_ref[...].T[:8, :lines]
    table_ref[...] = jnp.broadcast_to(turned[None], table_ref.shape)


def in_vmem(count):
    return [pl.BlockSpec(memory_space=pltpu.VMEM)] * count


def stats_of(z, kept, received, teacher, target, members):
    cut, columns = kept[0].shape[1:]
    chips = len(PLACE)
    lines = chips * cut
    padded = -(-lines // 128) * 128
    return call(
        stats_kernel,
        20 * lines * columns,
        14 * lines * columns,
        in_specs=[pl.BlockSpec(memory_space=pltpu.SMEM)] + in_vmem(2 * len(BATCHES) + 2),
        out_specs=in_vmem(2),
        out_shape=[
            jax.ShapeDtypeStruct((chips, cut, columns), F32),
            jax.ShapeDtypeStruct((members, 8, lines), F32),
        ],
        scratch_shapes=[pltpu.VMEM((padded, 128), F32)],
    )(z, *kept, *received, teacher, target)


def merged(table):
    max_s = jnp.max(table[:, 0], axis=0, keepdims=True)
    max_t = jnp.max(table[:, 3], axis=0, keepdims=True)
    scale_s = jnp.exp(table[:, 0] - max_s)
    scale_t = jnp.exp(table[:, 3] - max_t)

    def total(value):
        return jnp.sum(value, axis=0, keepdims=True)

    return [
        max_s,
        total(table[:, 1] * scale_s),
        total(table[:, 2] * scale_s),
        max_t,
        total(table[:, 4] * scale_t),
        total(table[:, 5]),
        total(table[:, 6]),
    ]


def merge_kernel(table_ref, out_ref):
    rows = merged(table_ref[...])
    table = jnp.concatenate(rows + [jnp.zeros_like(rows[0])], axis=0)
    out_ref[...] = jnp.broadcast_to(table[None], out_ref.shape)


def merge_of(table, members):
    lines = table.shape[2]
    return call(
        merge_kernel,
        16 * table.size,
        8 * table.size,
        out_shape=jax.ShapeDtypeStruct((members, 8, lines), F32),
    )(table)


def grad_kernel(place_ref, logits_ref, *refs):
    count = len(BATCHES)
    sent, received_ref = refs[:count], refs[count]
    teacher_ref, table_ref, weight_ref, own_ref, partner_ref, rows_ref, columns_ref = refs[count + 1 :]
    cut, columns = logits_ref.shape[1:]
    lines = cut * len(PLACE)
    padded = columns_ref.shape[1]
    members = table_ref.shape[0] // 2
    sec = place_ref[1]
    for i in range(2):
        which = sec if i == 0 else 1 - sec
        max_s, sum_s, cross, max_t, sum_t, pick_s, pick_t = merged(
            table_ref[pl.ds(which * members, members)]
        )
        student = max_s + jnp.log(sum_s)
        taught = max_t + jnp.log(sum_t)
        kl = cross / sum_s - student + taught
        gap = pick_s - student - (pick_t - taught)
        zero = jnp.zeros_like(kl)
        table = jnp.concatenate(
            [kl, gap, student, taught, weight_ref[i], zero, zero, zero], axis=0
        )
        rows_ref[which] = table
        table = jnp.concatenate([table, jnp.zeros((120, lines), F32)], axis=0)
        if padded > lines:
            table = jnp.concatenate([table, jnp.zeros((128, padded - lines), F32)], axis=1)
        columns_ref[i] = table.T

    def grad(logits, teacher, row):
        log_student = logits - row[:, 2:3]
        log_teacher = teacher - row[:, 3:4]
        return row[:, 4:5] * jnp.exp(log_student) * (log_student - log_teacher - row[:, 0:1])

    place = 0
    for b, batch in enumerate(BATCHES):
        for i, k in enumerate(batch):
            chip = lax.rem(place_ref[0] + k, len(PLACE))
            at = pl.ds(pl.multiple_of(chip * cut, 8), cut)
            teacher = teacher_ref[place].astype(F32)
            mine = grad(logits_ref[place], teacher[:cut], columns_ref[0, at, :])
            theirs = grad(sent[b][i] + received_ref[place], teacher[cut:], columns_ref[1, at, :])
            both = jnp.concatenate([mine, theirs], axis=0).astype(BF16)
            own_ref[place] = both[:, : columns // 2]
            partner_ref[place] = both[:, columns // 2 :]
            place += 1


def grad_of(place, logits, sent, received, teacher, table, weight):
    chips, cut, columns = logits.shape
    lines = chips * cut
    padded = -(-lines // 128) * 128
    half = jax.ShapeDtypeStruct((chips, 2 * cut, columns // 2), BF16)
    return call(
        grad_kernel,
        20 * lines * columns,
        20 * lines * columns,
        in_specs=[pl.BlockSpec(memory_space=pltpu.SMEM)] + in_vmem(len(BATCHES) + 5),
        out_specs=in_vmem(3),
        out_shape=[half, half, jax.ShapeDtypeStruct((2, 8, lines), F32)],
        scratch_shapes=[pltpu.VMEM((2, padded, 128), F32)],
    )(place, logits, *sent, received, teacher, table, weight)


def terms_kernel(own_grad_ref, partner_grad_ref, own_ref, partner_ref, out_ref):
    terms = lax.dot_general(own_ref[...], own_grad_ref[...], NT, preferred_element_type=F32)
    terms += lax.dot_general(
        partner_ref[...], partner_grad_ref[...], NT, preferred_element_type=F32
    )
    out_ref[0] = terms.astype(BF16)


def terms_of(own_grad, partner_grad, own, partner, members):
    chips, size, columns = own_grad.shape
    depth = own.shape[0]
    lines = chips * size
    width = depth // members
    weights = pl.BlockSpec((width, columns), lambda i: (i, 0))
    return call(
        terms_kernel,
        4 * lines * columns * depth,
        4 * (lines + depth) * columns + 2 * lines * depth,
        grid=(members,),
        in_specs=[whole((lines, columns))] * 2 + [weights] * 2,
        out_specs=pl.BlockSpec((1, width, lines), lambda i: (i, 0, 0)),
        out_shape=jax.ShapeDtypeStruct((members, width, lines), BF16),
    )(own_grad.reshape(lines, columns), partner_grad.reshape(lines, columns), own, partner)


def sum_kernel(place_ref, parts_ref, out_ref):
    size = out_ref.shape[1]
    total = None
    for member in range(parts_ref.shape[0]):
        term = parts_ref[member].astype(F32)
        total = term if total is None else total + term
    total = total.T.astype(BF16)
    for i, k in enumerate(PLACE):
        chip = lax.rem(place_ref[0] + k, len(PLACE))
        out_ref[chip] = total[i * size : (i + 1) * size]


def sum_of(place, parts):
    members, width, lines = parts.shape
    chips = len(PLACE)
    return call(
        sum_kernel,
        parts.size,
        2 * parts.size,
        in_specs=[pl.BlockSpec(memory_space=pltpu.SMEM)] + in_vmem(1),
        out_specs=in_vmem(1)[0],
        out_shape=jax.ShapeDtypeStruct((chips, lines // chips, width), BF16),
    )(place, parts)


def head_grad_kernel(a_rows_ref, b_rows_ref, a_grad_ref, b_grad_ref, out_ref):
    terms = lax.dot_general(a_rows_ref[...], a_grad_ref[...], TN, preferred_element_type=F32)
    terms += lax.dot_general(b_rows_ref[...], b_grad_ref[...], TN, preferred_element_type=F32)
    out_ref[...] = terms.astype(BF16)


def head_grad_of(a_rows, b_rows, a_grad, b_grad):
    lines, depth = a_rows.shape
    columns = a_grad.shape[-1]
    tile = min(256, depth)
    rows = pl.BlockSpec((lines, tile), lambda i: (0, i))
    return call(
        head_grad_kernel,
        4 * lines * depth * columns,
        4 * (lines * depth + lines * columns) + 2 * depth * columns,
        grid=(depth // tile,),
        in_specs=[rows, rows, whole((lines, columns)), whole((lines, columns))],
        out_specs=pl.BlockSpec((tile, columns), lambda i: (i, 0)),
        out_shape=jax.ShapeDtypeStruct((depth, columns), BF16),
    )(a_rows, b_rows, a_grad.reshape(lines, columns), b_grad.reshape(lines, columns))


def exchange(copies, axis, groups=None):
    return lax.all_to_all(
        copies, axis, split_axis=0, concat_axis=0, tiled=True, axis_index_groups=groups
    )


def on_device(hidden, head, teacher_logits, loss_mask, token_ids, row_order):
    dp_size = lax.axis_size("dp")
    vocab_size = lax.axis_size("vocab")
    z_size = dp_size // 2
    far = z_size // 2
    sec = lax.axis_index("sec")
    dp = lax.axis_index("dp")
    vocab = lax.axis_index("vocab")
    z, core = dp // 2, dp % 2
    block_width = head.shape[1]
    rows, width = hidden.shape
    cut = rows // 2
    lines = z_size * cut
    teacher_rows = teacher_logits.shape[0]
    swap_sec = [(0, 1), (1, 0)]
    swap_core = [(i, i ^ 1) for i in range(dp_size)]
    along = [[2 * i + c for i in range(z_size)] for c in range(2)]

    def shift(by):
        return [(i, (i + 2 * by) % dp_size) for i in range(dp_size)]

    def to_partner(value):
        return lax.ppermute(value, "dp", swap_core)

    head_partner = to_partner(head)
    arranged = jnp.where(sec == 0, hidden, jnp.concatenate([hidden[cut:], hidden[:cut]], axis=0))
    copies = jnp.broadcast_to(arranged[None], (vocab_size, rows, width))
    features = exchange(copies, "vocab").transpose(1, 0, 2).reshape(rows, vocab_size * width)

    tiles = teacher_logits.reshape(teacher_rows, 2, vocab_size, block_width)
    tiles = jnp.where(core == 0, tiles, jnp.concatenate([tiles[:, 1:], tiles[:, :1]], axis=1))
    tiles, features = lax.optimization_barrier((tiles, features))
    tiles = lax.all_to_all(tiles, "vocab", split_axis=2, concat_axis=1, tiled=True)
    tiles = tiles.reshape(teacher_rows, z_size, 2 * block_width)

    blocks = {0: [features]}
    kept, sent, received = [], [], []

    def take(batch, *before):
        mine, theirs = logits_of([blocks[k] for k in batch], head, head_partner)
        kept.append(mine)
        sent.append(theirs)
        if before:
            theirs = lax.optimization_barrier((theirs,) + before)[0]
        received.append(lax.ppermute(theirs, "sec", swap_sec))

    up, down = features, features
    middle = features.shape[1] // 2
    for step in range(1, far):
        up = lax.ppermute(up, "dp", shift(1))
        down = lax.ppermute(down, "dp", shift(-1))
        blocks[step], blocks[z_size - step] = [down], [up]
        if step == 1:
            up, down, tiles = lax.optimization_barrier((up, down, tiles))
        if step == 2:
            up, down, kept[0] = lax.optimization_barrier((up, down, kept[0]))
        if step < far - 1:
            take(BATCHES[step - 1])
    blocks[far] = [
        lax.ppermute(up[:, :middle], "dp", shift(1)),
        lax.ppermute(down[:, middle:], "dp", shift(-1)),
    ]
    blocks[far], received[0] = lax.optimization_barrier((blocks[far], received[0]))
    take(BATCHES[2])
    tiles = lax.optimization_barrier((tiles, kept[2], received[1]))[0]
    teacher = lax.all_to_all(
        tiles, "dp", split_axis=1, concat_axis=0, tiled=True, axis_index_groups=along
    ).reshape(lines, 2 * block_width)
    teacher = lax.optimization_barrier((teacher, received[2]))[0]
    teacher_across = lax.ppermute(teacher, "sec", swap_sec)

    chips = (z + jnp.array(PLACE, jnp.int32)) % z_size
    line = jnp.arange(cut, dtype=jnp.int32)

    def tokens_at(chip, which):
        return (((chip * 2 + core) * rows + which * cut)[:, None] + line).astype(jnp.int32)

    token = jnp.concatenate([tokens_at(chips, sec), tokens_at(chips, 1 - sec)], axis=1)
    by_device = row_order.reshape(2, z_size, 2, teacher_rows)

    def order_of(section, parity):
        part = lax.dynamic_index_in_dim(by_device, section, 0, keepdims=False)
        return lax.dynamic_index_in_dim(part, parity, 1, keepdims=False).reshape(-1)

    order = jnp.concatenate(
        [order_of(a, c) for c in (core, 1 - core) for a in (sec, 1 - sec)]
    )
    taught = aligned(
        order[None, :],
        token.reshape(-1, 1),
        (teacher, teacher_across),
        (to_partner(teacher), to_partner(teacher_across)),
    ).reshape(z_size, rows, 2 * block_width)

    ids = jnp.take(token_ids, tokens_at(chips, sec))
    from_own = ids - ((2 * z + core) * vocab_size + vocab) * block_width
    from_partner = ids - ((2 * z + 1 - core) * vocab_size + vocab) * block_width

    def inside(value):
        return (value >= 0) & (value < block_width)

    target = jnp.where(
        inside(from_own), from_own, jnp.where(inside(from_partner), from_partner + block_width, -1)
    )
    place = jnp.stack([z, sec]).astype(jnp.int32)
    logits, table = stats_of(place, kept, received, taught, target[:, :, None], z_size)
    table = exchange(merge_of(exchange(table, "dp", along), 2 * vocab_size), ("sec", "vocab"))

    held = lax.optimization_barrier(jnp.concatenate(kept, axis=0))
    held = lax.optimization_barrier((held, received[2], teacher_across))[0]
    returned = lax.ppermute(held, "sec", swap_sec)

    every = jnp.arange(z_size, dtype=jnp.int32)
    weight = jnp.stack(
        [jnp.take(loss_mask, tokens_at(every, a)).reshape(1, lines) for a in (sec, 1 - sec)]
    ).astype(F32)
    own_grad, partner_grad, per_row = grad_of(
        place, logits, sent, returned, taught, table, weight
    )

    terms = terms_of(own_grad, partner_grad, head, head_partner, vocab_size)
    by_chip = sum_of(place, exchange(terms, "vocab"))
    own_rows = jnp.concatenate([jnp.concatenate(blocks[k], axis=1) for k in PLACE], axis=0)
    head_grad = head_grad_of(
        own_rows, to_partner(own_rows), own_grad, to_partner(partner_grad)
    )

    by_chip, head_grad = lax.optimization_barrier((by_chip, head_grad))
    hidden_grad = jnp.sum(exchange(by_chip, "dp", along).astype(F32), axis=0)
    hidden_grad = jnp.where(
        sec == 0, hidden_grad, jnp.concatenate([hidden_grad[cut:], hidden_grad[:cut]], axis=0)
    )

    other_rows = to_partner(per_row)
    per_row = jnp.where(z % 2 == core, per_row, other_rows)
    per_row = lax.dynamic_index_in_dim(per_row, core, 0, keepdims=False)
    per_row = lax.dynamic_slice_in_dim(per_row, (sec * (z_size // 2) + z // 2) * cut, cut, 1)
    return (head_grad, hidden_grad, per_row[0], per_row[1])


def solution(mesh):
    in_specs = (
        P("dp", ("sec", "vocab")),
        P("sec", ("dp", "vocab")),
        P(("sec", "dp"), "vocab"),
        P(),
        P(),
        P(),
    )
    out_specs = (
        P("sec", ("dp", "vocab")),
        P("dp", ("sec", "vocab")),
        P(("sec", "dp")),
        P(("sec", "dp")),
    )
    return jax.shard_map(
        on_device, mesh=mesh, in_specs=in_specs, out_specs=out_specs, check_vma=False
    )
```

```python
import functools

import jax
import jax.numpy as jnp
from jax import lax
from jax.experimental import pallas as pl
from jax.experimental.pallas import tpu as pltpu
from jax.sharding import PartitionSpec as P

F32 = jnp.float32
BF16 = jnp.bfloat16
NT = (((1,), (1,)), ((), ()))
TN = (((0,), (0,)), ((), ()))
INTERP = False
VMEM_LIMIT = 16 * 1024 * 1024


def call(kernel, flops, traffic, **spec):
    return pl.pallas_call(
        kernel,
        compiler_params=pltpu.CompilerParams(vmem_limit_bytes=VMEM_LIMIT),
        cost_estimate=pl.CostEstimate(flops=flops, bytes_accessed=traffic, transcendentals=0),
        interpret=INTERP,
        **spec,
    )


def whole(shape):
    return pl.BlockSpec(shape, lambda i: (0,) * len(shape))


BATCHES = ((0, 1, 7), (2, 6), (3, 4, 5))
PLACE = tuple(k for batch in BATCHES for k in batch)


def logits_kernel(parts, *refs):
    row_refs, (own_ref, partner_ref, mine_ref, theirs_ref) = refs[:-4], refs[-4:]
    blocks, at = [], 0
    for count in parts:
        blocks.append(jnp.concatenate([ref[...] for ref in row_refs[at : at + count]], axis=1))
        at += count
    rows = jnp.concatenate(blocks, axis=0)
    size = blocks[0].shape[0]
    cut = size // 2
    columns = own_ref.shape[1]
    for base, ref in ((0, own_ref), (columns, partner_ref)):
        for first in range(0, columns, 256):
            last = min(first + 256, columns)
            terms = jnp.dot(rows, ref[:, first:last], preferred_element_type=F32)
            for i in range(len(parts)):
                mine_ref[i, :, base + first : base + last] = terms[i * size : i * size + cut]
                theirs_ref[i, :, base + first : base + last] = terms[
                    i * size + cut : (i + 1) * size
                ]


def logits_of(blocks, own, partner):
    depth, columns = own.shape
    size = blocks[0][0].shape[0]
    flat = [piece for block in blocks for piece in block]
    count = len(blocks)
    out = jax.ShapeDtypeStruct((count, size // 2, 2 * columns), F32)
    return call(
        functools.partial(logits_kernel, tuple(len(block) for block in blocks)),
        4 * count * size * depth * columns,
        4 * depth * columns + 8 * count * size * columns,
        in_specs=in_vmem(len(flat) + 2),
        out_specs=in_vmem(2),
        out_shape=[out, out],
    )(*flat, own, partner)


def align_kernel(order_ref, token_ref, a_ref, b_ref, c_ref, d_ref, out_ref, choice_ref):
    lines = a_ref.shape[0]

    @pl.when(pl.program_id(0) == 0)
    def _():
        choice_ref[...] = jnp.where(order_ref[...] == token_ref[...], 1.0, 0.0).astype(BF16)

    total = None
    for i, ref in enumerate((a_ref, b_ref, c_ref, d_ref)):
        choice = choice_ref[:, i * lines : (i + 1) * lines]
        term = jnp.dot(choice, ref[...], preferred_element_type=F32)
        total = term if total is None else total + term
    out_ref[...] = total.astype(BF16)


def aligned(order, token, own, swapped):
    lines, columns = own[0].shape
    tiles = 2
    tile = columns // tiles
    here = pl.BlockSpec((lines, tile), lambda i: (0, i))
    there = pl.BlockSpec((lines, tile), lambda i: (0, lax.rem(i + tiles // 2, tiles)))
    tokens = token.shape[0]
    return call(
        align_kernel,
        8 * tokens * lines * columns,
        12 * lines * columns,
        grid=(tiles,),
        in_specs=[whole(order.shape), whole(token.shape), here, here, there, there],
        out_specs=pl.BlockSpec((tokens, tile), lambda i: (0, i)),
        out_shape=jax.ShapeDtypeStruct((tokens, columns), BF16),
        scratch_shapes=[pltpu.VMEM((tokens, 4 * lines), BF16)],
    )(order, token, *own, *swapped)


def stats_kernel(z_ref, *refs):
    count = len(BATCHES)
    kept, received = refs[:count], refs[count : 2 * count]
    teacher_ref, target_ref, logits_ref, table_ref, columns_ref = refs[2 * count :]
    cut = kept[0].shape[1]
    lane = lax.broadcasted_iota(jnp.int32, (cut, 128), 1)

    def total(value):
        return jnp.sum(value, axis=1, keepdims=True)

    place = 0
    for b, batch in enumerate(BATCHES):
        for i, k in enumerate(batch):
            logits = kept[b][i] + received[b][i]
            logits_ref[place] = logits
            teacher = teacher_ref[place].astype(F32)[:cut]
            hit = lax.broadcasted_iota(jnp.int32, logits.shape, 1) == target_ref[place]
            top_s = jnp.max(logits, axis=1, keepdims=True)
            top_t = jnp.max(teacher, axis=1, keepdims=True)
            exp_s = jnp.exp(logits - top_s)
            columns = [
                top_s,
                total(exp_s),
                total(exp_s * (logits - teacher)),
                top_t,
                total(jnp.exp(teacher - top_t)),
                total(jnp.where(hit, logits, 0.0)),
                total(jnp.where(hit, teacher, 0.0)),
            ]
            table = jnp.zeros((cut, 128), F32)
            for j, column in enumerate(columns):
                table = jnp.where(lane == j, column, table)
            chip = lax.rem(z_ref[0] + k, len(PLACE))
            columns_ref[pl.ds(pl.multiple_of(chip * cut, 8), cut), :] = table
            place += 1
    lines = cut * len(PLACE)
    turned = columns_ref[...].T[:8, :lines]
    table_ref[...] = jnp.broadcast_to(turned[None], table_ref.shape)


def in_vmem(count):
    return [pl.BlockSpec(memory_space=pltpu.VMEM)] * count


def stats_of(z, kept, received, teacher, target, members):
    cut, columns = kept[0].shape[1:]
    chips = len(PLACE)
    lines = chips * cut
    padded = -(-lines // 128) * 128
    return call(
        stats_kernel,
        20 * lines * columns,
        14 * lines * columns,
        in_specs=[pl.BlockSpec(memory_space=pltpu.SMEM)] + in_vmem(2 * len(BATCHES) + 2),
        out_specs=in_vmem(2),
        out_shape=[
            jax.ShapeDtypeStruct((chips, cut, columns), F32),
            jax.ShapeDtypeStruct((members, 8, lines), F32),
        ],
        scratch_shapes=[pltpu.VMEM((padded, 128), F32)],
    )(z, *kept, *received, teacher, target)


def merged(table):
    max_s = jnp.max(table[:, 0], axis=0, keepdims=True)
    max_t = jnp.max(table[:, 3], axis=0, keepdims=True)
    scale_s = jnp.exp(table[:, 0] - max_s)
    scale_t = jnp.exp(table[:, 3] - max_t)

    def total(value):
        return jnp.sum(value, axis=0, keepdims=True)

    return [
        max_s,
        total(table[:, 1] * scale_s),
        total(table[:, 2] * scale_s),
        max_t,
        total(table[:, 4] * scale_t),
        total(table[:, 5]),
        total(table[:, 6]),
    ]


def merge_kernel(table_ref, out_ref):
    rows = merged(table_ref[...])
    table = jnp.concatenate(rows + [jnp.zeros_like(rows[0])], axis=0)
    out_ref[...] = jnp.broadcast_to(table[None], out_ref.shape)


def merge_of(table, members):
    lines = table.shape[2]
    return call(
        merge_kernel,
        16 * table.size,
        8 * table.size,
        out_shape=jax.ShapeDtypeStruct((members, 8, lines), F32),
    )(table)


def grad_kernel(place_ref, logits_ref, *refs):
    count = len(BATCHES)
    sent, received_ref = refs[:count], refs[count]
    teacher_ref, table_ref, weight_ref, own_ref, partner_ref, rows_ref, columns_ref = refs[count + 1 :]
    cut, columns = logits_ref.shape[1:]
    lines = cut * len(PLACE)
    padded = columns_ref.shape[1]
    members = table_ref.shape[0] // 2
    sec = place_ref[1]
    for i in range(2):
        which = sec if i == 0 else 1 - sec
        max_s, sum_s, cross, max_t, sum_t, pick_s, pick_t = merged(
            table_ref[pl.ds(which * members, members)]
        )
        student = max_s + jnp.log(sum_s)
        taught = max_t + jnp.log(sum_t)
        kl = cross / sum_s - student + taught
        gap = pick_s - student - (pick_t - taught)
        zero = jnp.zeros_like(kl)
        table = jnp.concatenate(
            [kl, gap, student, taught, weight_ref[i], zero, zero, zero], axis=0
        )
        rows_ref[which] = table
        table = jnp.concatenate([table, jnp.zeros((120, lines), F32)], axis=0)
        if padded > lines:
            table = jnp.concatenate([table, jnp.zeros((128, padded - lines), F32)], axis=1)
        columns_ref[i] = table.T

    def grad(logits, teacher, row):
        log_student = logits - row[:, 2:3]
        log_teacher = teacher - row[:, 3:4]
        return row[:, 4:5] * jnp.exp(log_student) * (log_student - log_teacher - row[:, 0:1])

    place = 0
    for b, batch in enumerate(BATCHES):
        for i, k in enumerate(batch):
            chip = lax.rem(place_ref[0] + k, len(PLACE))
            at = pl.ds(pl.multiple_of(chip * cut, 8), cut)
            teacher = teacher_ref[place].astype(F32)
            mine = grad(logits_ref[place], teacher[:cut], columns_ref[0, at, :])
            theirs = grad(sent[b][i] + received_ref[place], teacher[cut:], columns_ref[1, at, :])
            both = jnp.concatenate([mine, theirs], axis=0).astype(BF16)
            own_ref[place] = both[:, : columns // 2]
            partner_ref[place] = both[:, columns // 2 :]
            place += 1


def grad_of(place, logits, sent, received, teacher, table, weight):
    chips, cut, columns = logits.shape
    lines = chips * cut
    padded = -(-lines // 128) * 128
    half = jax.ShapeDtypeStruct((chips, 2 * cut, columns // 2), BF16)
    return call(
        grad_kernel,
        20 * lines * columns,
        20 * lines * columns,
        in_specs=[pl.BlockSpec(memory_space=pltpu.SMEM)] + in_vmem(len(BATCHES) + 5),
        out_specs=in_vmem(3),
        out_shape=[half, half, jax.ShapeDtypeStruct((2, 8, lines), F32)],
        scratch_shapes=[pltpu.VMEM((2, padded, 128), F32)],
    )(place, logits, *sent, received, teacher, table, weight)


def terms_kernel(own_grad_ref, partner_grad_ref, own_ref, partner_ref, out_ref):
    terms = lax.dot_general(own_ref[...], own_grad_ref[...], NT, preferred_element_type=F32)
    terms += lax.dot_general(
        partner_ref[...], partner_grad_ref[...], NT, preferred_element_type=F32
    )
    width = out_ref.shape[1]
    for i in range(out_ref.shape[0]):
        out_ref[i] = terms[i * width : (i + 1) * width].astype(BF16)


def terms_of(own_grad, partner_grad, own, partner, members):
    chips, size, columns = own_grad.shape
    depth = own.shape[0]
    lines = chips * size
    width = depth // members
    group = 2
    weights = pl.BlockSpec((group * width, columns), lambda i: (i, 0))
    return call(
        terms_kernel,
        4 * lines * columns * depth,
        4 * (lines + depth) * columns + 2 * lines * depth,
        grid=(members // group,),
        in_specs=[whole((lines, columns))] * 2 + [weights] * 2,
        out_specs=pl.BlockSpec((group, width, lines), lambda i: (i, 0, 0)),
        out_shape=jax.ShapeDtypeStruct((members, width, lines), BF16),
    )(own_grad.reshape(lines, columns), partner_grad.reshape(lines, columns), own, partner)


def sum_kernel(place_ref, parts_ref, out_ref):
    size = out_ref.shape[1]
    total = None
    for member in range(parts_ref.shape[0]):
        term = parts_ref[member].astype(F32)
        total = term if total is None else total + term
    total = total.T.astype(BF16)
    for i, k in enumerate(PLACE):
        chip = lax.rem(place_ref[0] + k, len(PLACE))
        out_ref[chip] = total[i * size : (i + 1) * size]


def sum_of(place, parts):
    members, width, lines = parts.shape
    chips = len(PLACE)
    return call(
        sum_kernel,
        parts.size,
        2 * parts.size,
        in_specs=[pl.BlockSpec(memory_space=pltpu.SMEM)] + in_vmem(1),
        out_specs=in_vmem(1)[0],
        out_shape=jax.ShapeDtypeStruct((chips, lines // chips, width), BF16),
    )(place, parts)


def head_grad_kernel(a_rows_ref, b_rows_ref, a_grad_ref, b_grad_ref, out_ref):
    terms = lax.dot_general(a_rows_ref[...], a_grad_ref[...], TN, preferred_element_type=F32)
    terms += lax.dot_general(b_rows_ref[...], b_grad_ref[...], TN, preferred_element_type=F32)
    out_ref[...] = terms.astype(BF16)


def head_grad_of(a_rows, b_rows, a_grad, b_grad):
    lines, depth = a_rows.shape
    columns = a_grad.shape[-1]
    tile = min(256, depth)
    rows = pl.BlockSpec((lines, tile), lambda i: (0, i))
    return call(
        head_grad_kernel,
        4 * lines * depth * columns,
        4 * (lines * depth + lines * columns) + 2 * depth * columns,
        grid=(depth // tile,),
        in_specs=[rows, rows, whole((lines, columns)), whole((lines, columns))],
        out_specs=pl.BlockSpec((tile, columns), lambda i: (i, 0)),
        out_shape=jax.ShapeDtypeStruct((depth, columns), BF16),
    )(a_rows, b_rows, a_grad.reshape(lines, columns), b_grad.reshape(lines, columns))


def exchange(copies, axis, groups=None):
    return lax.all_to_all(
        copies, axis, split_axis=0, concat_axis=0, tiled=True, axis_index_groups=groups
    )


def on_device(hidden, head, teacher_logits, loss_mask, token_ids, row_order):
    dp_size = lax.axis_size("dp")
    vocab_size = lax.axis_size("vocab")
    z_size = dp_size // 2
    far = z_size // 2
    sec = lax.axis_index("sec")
    dp = lax.axis_index("dp")
    vocab = lax.axis_index("vocab")
    z, core = dp // 2, dp % 2
    block_width = head.shape[1]
    rows, width = hidden.shape
    cut = rows // 2
    lines = z_size * cut
    teacher_rows = teacher_logits.shape[0]
    swap_sec = [(0, 1), (1, 0)]
    swap_core = [(i, i ^ 1) for i in range(dp_size)]
    along = [[2 * i + c for i in range(z_size)] for c in range(2)]

    def shift(by):
        return [(i, (i + 2 * by) % dp_size) for i in range(dp_size)]

    def to_partner(value):
        return lax.ppermute(value, "dp", swap_core)

    head_partner = to_partner(head)
    arranged = jnp.where(sec == 0, hidden, jnp.concatenate([hidden[cut:], hidden[:cut]], axis=0))
    copies = jnp.broadcast_to(arranged[None], (vocab_size, rows, width))
    features = exchange(copies, "vocab").transpose(1, 0, 2).reshape(rows, vocab_size * width)

    tiles = teacher_logits.reshape(teacher_rows, 2, vocab_size, block_width)
    tiles = jnp.where(core == 0, tiles, jnp.concatenate([tiles[:, 1:], tiles[:, :1]], axis=1))
    tiles, features = lax.optimization_barrier((tiles, features))
    tiles = lax.all_to_all(tiles, "vocab", split_axis=2, concat_axis=1, tiled=True)
    tiles = tiles.reshape(teacher_rows, z_size, 2 * block_width)

    blocks = {0: [features]}
    kept, sent, received = [], [], []

    def take(batch, *before):
        mine, theirs = logits_of([blocks[k] for k in batch], head, head_partner)
        kept.append(mine)
        sent.append(theirs)
        if before:
            theirs = lax.optimization_barrier((theirs,) + before)[0]
        received.append(lax.ppermute(theirs, "sec", swap_sec))

    up, down = features, features
    middle = features.shape[1] // 2
    for step in range(1, far):
        up = lax.ppermute(up, "dp", shift(1))
        down = lax.ppermute(down, "dp", shift(-1))
        blocks[step], blocks[z_size - step] = [down], [up]
        if step == 1:
            up, down, tiles = lax.optimization_barrier((up, down, tiles))
        if step == 2:
            up, down, kept[0] = lax.optimization_barrier((up, down, kept[0]))
        if step < far - 1:
            take(BATCHES[step - 1])
    blocks[far] = [
        lax.ppermute(up[:, :middle], "dp", shift(1)),
        lax.ppermute(down[:, middle:], "dp", shift(-1)),
    ]
    blocks[far], received[0] = lax.optimization_barrier((blocks[far], received[0]))
    take(BATCHES[2])
    tiles = lax.optimization_barrier((tiles, kept[2], received[1]))[0]
    teacher = lax.all_to_all(
        tiles, "dp", split_axis=1, concat_axis=0, tiled=True, axis_index_groups=along
    ).reshape(lines, 2 * block_width)
    teacher = lax.optimization_barrier((teacher, received[2]))[0]
    teacher_across = lax.ppermute(teacher, "sec", swap_sec)

    chips = (z + jnp.array(PLACE, jnp.int32)) % z_size
    line = jnp.arange(cut, dtype=jnp.int32)

    def tokens_at(chip, which):
        return (((chip * 2 + core) * rows + which * cut)[:, None] + line).astype(jnp.int32)

    token = jnp.concatenate([tokens_at(chips, sec), tokens_at(chips, 1 - sec)], axis=1)
    by_device = row_order.reshape(2, z_size, 2, teacher_rows)

    def order_of(section, parity):
        part = lax.dynamic_index_in_dim(by_device, section, 0, keepdims=False)
        return lax.dynamic_index_in_dim(part, parity, 1, keepdims=False).reshape(-1)

    order = jnp.concatenate(
        [order_of(a, c) for c in (core, 1 - core) for a in (sec, 1 - sec)]
    )
    taught = aligned(
        order[None, :],
        token.reshape(-1, 1),
        (teacher, teacher_across),
        (to_partner(teacher), to_partner(teacher_across)),
    ).reshape(z_size, rows, 2 * block_width)

    ids = jnp.take(token_ids, tokens_at(chips, sec))
    from_own = ids - ((2 * z + core) * vocab_size + vocab) * block_width
    from_partner = ids - ((2 * z + 1 - core) * vocab_size + vocab) * block_width

    def inside(value):
        return (value >= 0) & (value < block_width)

    target = jnp.where(
        inside(from_own), from_own, jnp.where(inside(from_partner), from_partner + block_width, -1)
    )
    place = jnp.stack([z, sec]).astype(jnp.int32)
    logits, table = stats_of(place, kept, received, taught, target[:, :, None], z_size)
    table = exchange(merge_of(exchange(table, "dp", along), 2 * vocab_size), ("sec", "vocab"))

    held = lax.optimization_barrier(jnp.concatenate(kept, axis=0))
    held = lax.optimization_barrier((held, received[2], teacher_across))[0]
    returned = lax.ppermute(held, "sec", swap_sec)

    every = jnp.arange(z_size, dtype=jnp.int32)
    weight = jnp.stack(
        [jnp.take(loss_mask, tokens_at(every, a)).reshape(1, lines) for a in (sec, 1 - sec)]
    ).astype(F32)
    own_grad, partner_grad, per_row = grad_of(
        place, logits, sent, returned, taught, table, weight
    )

    terms = terms_of(own_grad, partner_grad, head, head_partner, vocab_size)
    by_chip = sum_of(place, exchange(terms, "vocab"))
    own_rows = jnp.concatenate([jnp.concatenate(blocks[k], axis=1) for k in PLACE], axis=0)
    head_grad = head_grad_of(
        own_rows, to_partner(own_rows), own_grad, to_partner(partner_grad)
    )

    by_chip, head_grad = lax.optimization_barrier((by_chip, head_grad))
    hidden_grad = jnp.sum(exchange(by_chip, "dp", along).astype(F32), axis=0)
    hidden_grad = jnp.where(
        sec == 0, hidden_grad, jnp.concatenate([hidden_grad[cut:], hidden_grad[:cut]], axis=0)
    )

    other_rows = to_partner(per_row)
    per_row = jnp.where(z % 2 == core, per_row, other_rows)
    per_row = lax.dynamic_index_in_dim(per_row, core, 0, keepdims=False)
    per_row = lax.dynamic_slice_in_dim(per_row, (sec * (z_size // 2) + z // 2) * cut, cut, 1)
    return (head_grad, hidden_grad, per_row[0], per_row[1])


def solution(mesh):
    in_specs = (
        P("dp", ("sec", "vocab")),
        P("sec", ("dp", "vocab")),
        P(("sec", "dp"), "vocab"),
        P(),
        P(),
        P(),
    )
    out_specs = (
        P("sec", ("dp", "vocab")),
        P("dp", ("sec", "vocab")),
        P(("sec", "dp")),
        P(("sec", "dp")),
    )
    return jax.shard_map(
        on_device, mesh=mesh, in_specs=in_specs, out_specs=out_specs, check_vma=False
    )
```
